32 devices in a mesh: groups: 2 (over x), grid: 4 (over y, core), head: 4 (over z).
Axes of the slice: x: 2, y: 2, z: 4, core: 2. Of those that a mesh axis runs over, the one named last changes fastest.
Arguments:
- grid_x: bfloat16 [16384, 100], P(('groups', 'grid')), parts along dimension 0, may hold values from -6 to 6
- mesh_h: bfloat16 [2048, 1024], P(('groups', 'grid')), parts along dimension 0, may hold values from -6 to 6
- w_in: bfloat16 [100, 1024], replicated, may hold values from -0.625 to 0.625
- w_q: bfloat16 [1024, 1024], P(None, 'head'), may hold values from -0.1875 to 0.1875
- w_kv: bfloat16 [1024, 2, 1024], P(None, None, 'head'), may hold values from -0.1875 to 0.1875
- w_o: bfloat16 [1024, 1024], P('head'), may hold values from -0.1875 to 0.1875
- w_pqkv: bfloat16 [1024, 3, 1024], P(None, None, 'head'), may hold values from -0.1875 to 0.1875
- w_po: bfloat16 [1024, 1024], P('head'), may hold values from -0.1875 to 0.1875
- edge_src: int32 [4, 4, 256], P('grid'), may hold values from 0 to 2047
- edge_dst: int32 [4, 4, 256], P('grid'), may hold values from 0 to 255
- edge_count: int32 [4, 4], P('grid'), may hold values from 1 to 256, as said below
- win_idx: int32 [1024, 32], P('grid'), may hold values from 0 to 255
- cot: bfloat16 [2048, 1024], P(('groups', 'grid')), parts along dimension 0, may hold values from -6 to 6
Outputs:
- hm_out: bfloat16 [2048, 1024], P(('groups', 'grid'), 'head'), parts along dimension 0
- grad_wkv: float32 [2048, 2, 1024], P(('groups', 'grid'), None, 'head'), parts along dimension 0
The draws below stay inside these ranges and needn't reach their ends.
There are 2 independent parts, one for each index of `groups`. The reference program is written for one: setup_inputs(seed, part) draws one part's arguments, and reference() takes and returns one part's arrays. A program takes and returns all parts, laid end to end along the dimension named above; an argument that names none is the same for every part. Nothing has to cross between parts.
Inputs may be any that keep to these rules, and one draw needn't show every extreme that they name: edge_src[s, r, e] is a row among the 2048 grid rows of grid block s. edge_dst[r, s, e] is a node among the 256 mesh nodes of mesh block r. edge_count[r, s] counts the live slots, from the first, of the edges from grid block s to mesh block r; in every draw one r has 256 live slots from every s. win_idx[i] names nodes of the mesh block of node i by their index in that block; repeats count as often as they appear.
All inputs are finite; a program needn't handle non-finite values.
Results may differ from the reference program's by a relative error of at most 0.029.
Values may be sent and summed in bfloat16 or wider, within the bound.
A program may use at most 64 MiB of HBM per device.

```python
import math
import jax
import jax.numpy as jnp
from jax import lax

D = 1024
HEADS = 16
C = 100
G_DEV = 2048
M_DEV = 256
CAP = 256
WIN = 32
HEAD_SIZE = 64
HEAD_COLS = 256
SENDERS = 4
GRID_ROWS = 8192
MESH_NODES = 1024


def draw_edge_count(key, part):
    key = jax.random.fold_in(key, 11)
    level_key, trim_key, full_key = jax.random.split(key, 3)
    level = jax.random.randint(level_key, (SENDERS, SENDERS), 0, 4)
    table = jnp.array([CAP, CAP // 2, CAP // 4, CAP // 8], dtype=jnp.int32)
    base = jnp.take(table, level) - jax.random.randint(trim_key, (SENDERS, SENDERS), 0, CAP // 16)
    busiest = jax.random.randint(full_key, (), 0, SENDERS)
    rows = lax.broadcasted_iota(jnp.int32, (SENDERS, SENDERS), 0)
    return jnp.where(rows == busiest, CAP, base).astype(jnp.int32)


def plant(drawn, key, least, largest):
    extent = drawn.shape
    index_at = [jax.random.randint(jax.random.fold_in(key, axis), (), 0, extent[axis]) for axis in range(len(extent))]
    drawn = drawn.at[tuple(index_at)].set(least)
    longest = extent.index(max(extent))
    index_at[longest] = (index_at[longest] + 1) % extent[longest]
    return drawn.at[tuple(index_at)].set(largest)


def block_scale(key, extent, pieces, smallest, top_value):
    def one(dim, parts):
        steps = jax.random.uniform(jax.random.fold_in(jax.random.fold_in(key, 6), dim), (parts,), jnp.float32, smallest / len(pieces), top_value / len(pieces))
        return jnp.repeat(jnp.exp(steps), extent[dim] // parts).reshape((-1,) + (1,) * (len(extent) - dim - 1))

    level = one(*pieces[0])
    for cut in pieces[1:]:
        level = level * one(*cut)
    return level


def noise(stream_key, extent, deviation, reach, pieces=(), kind=jnp.bfloat16):
    drawn = jax.random.normal(stream_key, extent, jnp.float32) * deviation
    if len(pieces) > 0:
        drawn = block_scale(stream_key, extent, pieces, -0.22, 0.18) * drawn
    return jnp.clip(drawn, min=-reach, max=reach).astype(kind)


def setup_inputs(seed: int = 0, part: int = 0) -> dict:
    seeds = jax.random.split(jax.random.key(seed), 14)
    part_splits = jax.random.split(jax.random.fold_in(seeds[13], part), 14)
    grid_x = noise(part_splits[0], (GRID_ROWS, C), 1.0, 6.0, ((0, 4),))
    mesh_h = noise(part_splits[1], (MESH_NODES, D), 1.0, 6.0, ((0, 4),))
    w_in = noise(seeds[2], (C, D), C ** -0.5, 0.625)
    w_q = noise(seeds[3], (D, D), D ** -0.5, 0.1875, ((1, 4),))
    w_kv = noise(seeds[4], (D, 2, D), D ** -0.5, 0.1875, ((2, 4),))
    w_o = noise(seeds[5], (D, D), D ** -0.5, 0.1875, ((0, 4),))
    w_pqkv = noise(seeds[6], (D, 3, D), D ** -0.5, 0.1875, ((2, 4),))
    w_po = noise(seeds[7], (D, D), D ** -0.5, 0.1875, ((0, 4),))
    edge_src = plant(jax.random.randint(seeds[8], (SENDERS, SENDERS, CAP), 0, G_DEV), jax.random.fold_in(seeds[8], 1), 0, G_DEV - 1).astype(jnp.int32)
    edge_dst = plant(jax.random.randint(seeds[9], (SENDERS, SENDERS, CAP), 0, M_DEV), jax.random.fold_in(seeds[9], 1), 0, M_DEV - 1).astype(jnp.int32)
    edge_count = draw_edge_count(jax.random.fold_in(seeds[13], 71), part)
    win_idx = plant(jax.random.randint(seeds[11], (MESH_NODES, WIN), 0, M_DEV), jax.random.fold_in(seeds[11], 1), 0, M_DEV - 1).astype(jnp.int32)
    cot = noise(part_splits[12], (MESH_NODES, D), 1.0, 6.0, ((0, 4),))
    return {"grid_x": grid_x, "mesh_h": mesh_h, "w_in": w_in, "w_q": w_q, "w_kv": w_kv, "w_o": w_o, "w_pqkv": w_pqkv, "w_po": w_po, "edge_src": edge_src, "edge_dst": edge_dst, "edge_count": edge_count, "win_idx": win_idx, "cot": cot}


norm_eps = 1e-05
cap_limit = 30.0

def layer_norm(values):
    row_mean = lax.optimization_barrier(jnp.mean(values, axis=-1, keepdims=True))
    centred_input = values - row_mean
    var = lax.optimization_barrier(jnp.mean(centred_input * centred_input, axis=-1, keepdims=True))
    return centred_input * lax.rsqrt(var + norm_eps)

def matmul(left, right):
    return jnp.dot(left.astype(jnp.float32), right.astype(jnp.float32), preferred_element_type=jnp.float32)

def matmul_t(left, right):
    return lax.dot_general(left.astype(jnp.float32), right.astype(jnp.float32), (((1,), (1,)), ((), ())), preferred_element_type=jnp.float32)

def bf_round(values):
    return lax.optimization_barrier(values.astype(jnp.bfloat16)).astype(jnp.float32)

def rounded_partials(terms):
    return lax.optimization_barrier(jnp.sum(bf_round(terms), axis=0))

def reference(grid_x, mesh_h, w_in, w_q, w_kv, w_o, w_pqkv, w_po, edge_src, edge_dst, edge_count, win_idx, cot):
    float_value = jnp.float32
    bfloat_value = jnp.bfloat16
    n_grid = edge_count.shape[0]
    groups = D // HEAD_COLS
    scale = 1.0 / math.sqrt(HEAD_SIZE)
    kv_flat = w_kv.reshape(D, 2 * D)
    qkv_flat = w_pqkv.reshape(D, 3 * D)
    slot_live = (jnp.arange(CAP, dtype=jnp.int32)[None, None, :] < edge_count[:, :, None]).astype(float_value)
    sender_base = (jnp.arange(n_grid, dtype=jnp.int32) * G_DEV)[:, None]

    def one_block(total, block):
        start = block * M_DEV
        mesh_rows = lax.dynamic_slice_in_dim(mesh_h, start, M_DEV, 0).astype(float_value)
        mesh_normed = layer_norm(mesh_rows).astype(bfloat_value)
        query = matmul(mesh_normed, w_q).astype(bfloat_value)
        self_kv = matmul(mesh_normed, kv_flat).astype(bfloat_value)
        sources = (sender_base + lax.dynamic_index_in_dim(edge_src, block, 1, keepdims=False)).reshape(-1)
        dest = lax.dynamic_index_in_dim(edge_dst, block, 0, keepdims=False).reshape(-1)
        live = lax.dynamic_index_in_dim(slot_live, block, 0, keepdims=False).reshape(-1)
        slots = dest.shape[0]
        edge_normed = layer_norm(matmul(jnp.take(grid_x, sources, axis=0), w_in)).astype(bfloat_value)
        edge_kv = matmul(edge_normed, kv_flat).astype(bfloat_value)
        q_self = query.astype(float_value).reshape(M_DEV, HEADS, HEAD_SIZE)
        k_self = self_kv[:, :D].astype(float_value).reshape(M_DEV, HEADS, HEAD_SIZE)
        v_self = self_kv[:, D:].astype(float_value).reshape(M_DEV, HEADS, HEAD_SIZE)
        q_edge = jnp.take(q_self, dest, axis=0)
        k_edge = edge_kv[:, :D].astype(float_value).reshape(slots, HEADS, HEAD_SIZE)
        v_edge = edge_kv[:, D:].astype(float_value).reshape(slots, HEADS, HEAD_SIZE)
        tanh_edge = jnp.tanh(lax.optimization_barrier(jnp.sum(q_edge * k_edge, axis=2)) * scale / cap_limit)
        tanh_self = jnp.tanh(lax.optimization_barrier(jnp.sum(q_self * k_self, axis=2)) * scale / cap_limit)
        weight_edge = jnp.exp(cap_limit * tanh_edge) * live[:, None]
        weight_self = jnp.exp(cap_limit * tanh_self)
        denom = weight_self + jax.ops.segment_sum(weight_edge, dest, num_segments=M_DEV)
        prob_edge = weight_edge / jnp.take(denom, dest, axis=0)
        prob_self = weight_self / denom
        pe_round = bf_round(prob_edge)
        ps_round = bf_round(prob_self)
        mixed = (jax.ops.segment_sum(pe_round[:, :, None] * v_edge, dest, num_segments=M_DEV) + ps_round[:, :, None] * v_self).reshape(M_DEV, D).astype(bfloat_value)
        enc_terms = jnp.einsum('mjd,jde->jme', mixed.astype(float_value).reshape(M_DEV, groups, HEAD_COLS), w_o.astype(float_value).reshape(groups, HEAD_COLS, D))
        hm1 = mesh_rows + rounded_partials(enc_terms)
        row_mean = lax.optimization_barrier(jnp.mean(hm1, axis=1, keepdims=True))
        centred_input = hm1 - row_mean
        inverse_deviation = lax.rsqrt(lax.optimization_barrier(jnp.mean(centred_input * centred_input, axis=1, keepdims=True)) + norm_eps)
        normalized_input = centred_input * inverse_deviation
        processor_normed = normalized_input.astype(bfloat_value)
        qkv = matmul(processor_normed, qkv_flat).astype(bfloat_value)
        q2 = qkv[:, :D].astype(float_value).reshape(M_DEV, HEADS, HEAD_SIZE)
        k2 = qkv[:, D:2 * D].astype(float_value).reshape(M_DEV, HEADS, HEAD_SIZE)
        v2 = qkv[:, 2 * D:].astype(float_value).reshape(M_DEV, HEADS, HEAD_SIZE)
        window = lax.dynamic_slice_in_dim(win_idx, start, M_DEV, 0)
        members = lax.optimization_barrier(jnp.sum((window[:, :, None] == jnp.arange(M_DEV, dtype=jnp.int32)[None, None, :]).astype(float_value), axis=1))
        tanh2 = jnp.tanh(jnp.einsum('ihd,jhd->hij', q2, k2) * scale / cap_limit)
        weight2 = members[None] * jnp.exp(cap_limit * tanh2)
        prob2 = weight2 / lax.optimization_barrier(jnp.sum(weight2, axis=2, keepdims=True))
        p2_round = bf_round(prob2)
        attended = jnp.einsum('hij,jhd->ihd', p2_round, v2).reshape(M_DEV, D).astype(bfloat_value)
        out_terms = jnp.einsum('mjd,jde->jme', attended.astype(float_value).reshape(M_DEV, groups, HEAD_COLS), w_po.astype(float_value).reshape(groups, HEAD_COLS, D))
        hm_block = (hm1 + rounded_partials(out_terms)).astype(bfloat_value)
        cotangent_rows = lax.dynamic_slice_in_dim(cot, start, M_DEV, 0)
        d_att = matmul_t(cotangent_rows, w_po).astype(bfloat_value).astype(float_value).reshape(M_DEV, HEADS, HEAD_SIZE)
        dprob2 = jnp.einsum('ihd,jhd->hij', d_att, v2)
        dscore2 = prob2 * (dprob2 - lax.optimization_barrier(jnp.sum(prob2 * dprob2, axis=2, keepdims=True)))
        dz2 = bf_round(dscore2 * (1.0 - tanh2 * tanh2) * scale)
        d_q = jnp.einsum('hij,jhd->ihd', dz2, k2).astype(bfloat_value)
        d_k = jnp.einsum('hij,ihd->jhd', dz2, q2).astype(bfloat_value)
        d_v = jnp.einsum('hij,ihd->jhd', p2_round, d_att).astype(bfloat_value)
        d_qkv = jnp.stack([d_q.reshape(M_DEV, groups, HEAD_COLS), d_k.reshape(M_DEV, groups, HEAD_COLS), d_v.reshape(M_DEV, groups, HEAD_COLS)], axis=1)
        back_terms = jnp.einsum('mtjc,etjc->jme', d_qkv.astype(float_value), w_pqkv.astype(float_value).reshape(D, 3, groups, HEAD_COLS))
        normed_gradient = rounded_partials(back_terms)
        hidden_minus_gradient = (cotangent_rows.astype(float_value) + inverse_deviation * (normed_gradient - lax.optimization_barrier(jnp.mean(normed_gradient, axis=1, keepdims=True)) - normalized_input * lax.optimization_barrier(jnp.mean(normed_gradient * normalized_input, axis=1, keepdims=True)))).astype(bfloat_value)
        d_mixed = matmul_t(hidden_minus_gradient, w_o).astype(bfloat_value)
        dm_self = d_mixed.astype(float_value).reshape(M_DEV, HEADS, HEAD_SIZE)
        dm_edge = jnp.take(dm_self, dest, axis=0)
        dprob_edge = lax.optimization_barrier(jnp.sum(dm_edge * v_edge, axis=2))
        dprob_self = lax.optimization_barrier(jnp.sum(dm_self * v_self, axis=2))
        inner = prob_self * dprob_self + jax.ops.segment_sum(prob_edge * dprob_edge, dest, num_segments=M_DEV)
        dz_edge = prob_edge * (dprob_edge - jnp.take(inner, dest, axis=0)) * (1.0 - tanh_edge * tanh_edge) * scale
        dz_self = prob_self * (dprob_self - inner) * (1.0 - tanh_self * tanh_self) * scale
        edge_grad = jnp.concatenate([(dz_edge[:, :, None] * q_edge).reshape(slots, D), (pe_round[:, :, None] * dm_edge).reshape(slots, D)], axis=1).astype(bfloat_value)
        self_grad = jnp.concatenate([(dz_self[:, :, None] * q_self).reshape(M_DEV, D), (ps_round[:, :, None] * dm_self).reshape(M_DEV, D)], axis=1).astype(bfloat_value)
        dims = (((0,), (0,)), ((), ()))
        total = total + lax.dot_general(edge_normed.astype(float_value), edge_grad.astype(float_value), dims, preferred_element_type=float_value)
        total = total + lax.dot_general(mesh_normed.astype(float_value), self_grad.astype(float_value), dims, preferred_element_type=float_value)
        return (total, hm_block)
    total, blocks = lax.scan(one_block, jnp.zeros((D, 2 * D), jnp.float32), jnp.arange(n_grid, dtype=jnp.int32))
    return (blocks.reshape(n_grid * M_DEV, D), total.reshape(D, 2, D))
```

```python
import functools
import math

import jax
import jax.numpy as jnp
from jax import lax
from jax.experimental import pallas as pl
from jax.experimental.pallas import tpu as pltpu
from jax.sharding import PartitionSpec as P

HEAD_SIZE = 64
LANES = 128

norm_eps = 1e-05
cap_limit = 30.0
scale = 1.0 / math.sqrt(HEAD_SIZE)

f32 = jnp.float32
bf16 = jnp.bfloat16
MESH = pl.DeviceIdType.MESH


def normalize(values):
    row_mean = jnp.mean(values, axis=-1, keepdims=True)
    centred = values - row_mean
    var = jnp.mean(centred * centred, axis=-1, keepdims=True)
    inv = lax.rsqrt(var + norm_eps)
    return centred * inv, inv


def dot(a, b):
    return jnp.dot(a, b, preferred_element_type=f32)


def dot_t(a, b):
    return lax.dot_general(a, b, (((1,), (1,)), ((), ())), preferred_element_type=f32)


def t_dot(a, b):
    return lax.dot_general(a, b, (((0,), (0,)), ((), ())), preferred_element_type=f32)


def split(x):
    hi = x.astype(bf16)
    return hi, (x - hi.astype(f32)).astype(bf16)


def dot_split(a, x):
    hi, lo = split(x)
    return dot(a, hi) + dot(a, lo)


def kernel(
    n_grid,
    n_head,
    gx_ref,
    mesh_ref,
    w_in_ref,
    w_q_ref,
    w_kv_ref,
    w_o_ref,
    w_pqkv_ref,
    w_po_ref,
    src_ref,
    dst_ref,
    win_ref,
    cot_ref,
    hm_ref,
    grad_ref,
    rows_t,
    x_t,
    hot,
    hot_t,
    kv,
    tanh_e,
    prob_e,
    grads,
    q_s,
    kv_s,
    members,
    enc_send,
    enc_recv,
    normed,
    out_send,
    out_recv,
    hm_rows,
    hm_cols,
    back_send,
    back_recv,
    d_hm,
    grad_send,
    grad_recv,
    hs_sem,
    hr_sem,
    gs_sem,
    gr_sem,
):
    width = mesh_ref.shape[1]
    nodes = mesh_ref.shape[0]
    cols = w_q_ref.shape[1]
    cap = src_ref.shape[2]
    heads = cols // HEAD_SIZE
    own = nodes // n_head
    chunk = width // n_grid
    my_grid = lax.axis_index("grid")
    my_head = lax.axis_index("head")
    grid_peers = [lax.rem(my_grid + d, n_grid) for d in range(1, n_grid)]
    head_peers = [lax.rem(my_head + d, n_head) for d in range(1, n_head)]

    barrier = pltpu.get_barrier_semaphore()
    for peer in grid_peers:
        pl.semaphore_signal(barrier, inc=1, device_id={"grid": peer}, device_id_type=MESH)
    for peer in head_peers:
        pl.semaphore_signal(barrier, inc=1, device_id={"head": peer}, device_id_type=MESH)

    def send_grid(phase, d, src, dst):
        c = pltpu.make_async_remote_copy(
            src_ref=src,
            dst_ref=dst,
            send_sem=gs_sem.at[phase, d],
            recv_sem=gr_sem.at[phase, d],
            device_id={"grid": grid_peers[d]},
            device_id_type=MESH,
        )
        c.start()
        return c

    def send_head(phase, d, src, dst):
        c = pltpu.make_async_remote_copy(
            src_ref=src,
            dst_ref=dst,
            send_sem=hs_sem.at[phase, d],
            recv_sem=hr_sem.at[phase, d],
            device_id={"head": head_peers[d]},
            device_id_type=MESH,
        )
        c.start()
        return c

    def head_rows(peer):
        return pl.ds(pl.multiple_of(peer * own, own), own)

    def grid_rows(peer):
        return pl.ds(pl.multiple_of(peer * chunk, chunk), chunk)

    own_rows = head_rows(my_head)
    copies = []

    def gathered(peer):
        idx = src_ref[peer]
        total = None
        rows = gx_ref.shape[1]
        step = 512
        for start in range(0, rows, step):
            at = lax.broadcasted_iota(jnp.int32, (step, cap), 0) + start
            pick = jnp.where(at == idx, 1.0, 0.0).astype(bf16)
            part = dot(gx_ref[:, start : start + step], pick)
            total = part if total is None else total + part
        return total.astype(bf16)

    rows_t[n_grid] = gathered(grid_peers[0])
    pl.semaphore_wait(barrier, n_grid - 1 + n_head - 1)
    edge_copies = [send_grid(0, 0, rows_t.at[n_grid], rows_t.at[my_grid])]
    for d in range(1, n_grid - 1):
        rows_t[n_grid + d] = gathered(grid_peers[d])
        edge_copies.append(send_grid(0, d, rows_t.at[n_grid + d], rows_t.at[my_grid]))
    rows_t[my_grid] = gathered(my_grid)
    copies += edge_copies

    mesh_f = mesh_ref[...].astype(f32)
    mesh_n = normalize(mesh_f)[0]
    x_t[:, n_grid * cap : n_grid * cap + nodes] = mesh_n.T.astype(bf16)
    mesh_n = mesh_n.astype(bf16)
    q_s[...] = dot(mesh_n, w_q_ref[...]).astype(bf16)
    kv_s[...] = dot(mesh_n, w_kv_ref[...]).astype(bf16)

    def onehots(s, carry):
        at = lax.broadcasted_iota(jnp.int32, (nodes, cap), 0)
        pick = jnp.where(at == dst_ref[s], 1.0, 0.0)
        hot_t[s] = pick.astype(bf16)
        hot[s] = pick.T.astype(bf16)
        return carry

    lax.fori_loop(0, n_grid, onehots, 0)

    row_at = lax.shift_right_logical(lax.broadcasted_iota(jnp.int32, (cols, cols), 0), 6)
    col_at = lax.shift_right_logical(lax.broadcasted_iota(jnp.int32, (cols, cols), 1), 6)
    same_head = jnp.where(row_at == col_at, 1.0, 0.0).astype(bf16)

    def head_sum(x):
        hi, lo = split(x)
        return dot(hi, same_head) + dot(lo, same_head)

    for c in edge_copies:
        c.wait_recv()

    def embed(s, carry):
        row = normalize(t_dot(rows_t[s], w_in_ref[...]))[0]
        x_t[:, pl.ds(pl.multiple_of(s * cap, cap), cap)] = row.T.astype(bf16)
        kv[s] = dot(row.astype(bf16), w_kv_ref[...]).astype(bf16)
        return carry

    lax.fori_loop(0, n_grid, embed, 0)

    query = q_s[...]
    q_f = query.astype(f32)
    k_f = kv_s[:, :cols].astype(f32)
    v_f = kv_s[:, cols:].astype(f32)
    tanh_s = jnp.tanh(head_sum(q_f * k_f) * (scale / cap_limit))
    weight_s = jnp.exp(cap_limit * tanh_s)

    def scores(s, denom):
        q_e = dot(hot[s], query)
        t = jnp.tanh(head_sum(q_e * kv[s][:, :cols].astype(f32)) * (scale / cap_limit))
        w = jnp.exp(cap_limit * t)
        tanh_e[s] = t
        prob_e[s] = w
        return denom + dot_split(hot_t[s], w)

    denom = lax.fori_loop(0, n_grid, scores, weight_s)
    recip = 1.0 / denom
    prob_s = weight_s * recip
    recip_hi, recip_lo = split(recip)
    ps_b = prob_s.astype(bf16)

    def mix(s, total):
        p = prob_e[s] * (dot(hot[s], recip_hi) + dot(hot[s], recip_lo))
        prob_e[s] = p
        v = kv[s][:, cols:].astype(f32)
        return total + dot_split(hot_t[s], p.astype(bf16).astype(f32) * v)

    mixed = lax.fori_loop(0, n_grid, mix, ps_b.astype(f32) * v_f).astype(bf16)
    enc_send[...] = dot(mixed, w_o_ref[...]).astype(bf16)
    enc_copies = [
        send_head(0, d, enc_send.at[head_rows(head_peers[d])], enc_recv.at[d])
        for d in range(n_head - 1)
    ]
    copies += enc_copies

    lane = lax.broadcasted_iota(jnp.int32, (nodes, nodes), 1)
    win = win_ref[...]
    count = jnp.zeros((nodes, nodes), f32)
    for m in range(win.shape[1]):
        count = count + jnp.where(lane == win[:, m : m + 1], 1.0, 0.0)
    members[...] = count
    d_att = dot_t(cot_ref[...], w_po_ref[...]).astype(bf16)

    for c in enc_copies:
        c.wait_recv()
    enc_sum = enc_send[own_rows].astype(f32)
    for d in range(n_head - 1):
        enc_sum = enc_sum + enc_recv[d].astype(f32)
    hm1 = mesh_ref[own_rows].astype(f32) + enc_sum
    xhat, inv = normalize(hm1)
    normed[own_rows] = xhat.astype(bf16)
    norm_copies = [
        send_head(1, d, normed.at[own_rows], normed.at[own_rows]) for d in range(n_head - 1)
    ]
    copies += norm_copies
    for c in norm_copies:
        c.wait_recv()

    qkv = dot(normed[...], w_pqkv_ref[...]).astype(bf16)
    q2 = qkv[:, :cols]
    k2 = qkv[:, cols : 2 * cols]
    v2 = qkv[:, 2 * cols :]
    col_head = lax.shift_right_logical(lax.broadcasted_iota(jnp.int32, (nodes, cols), 1), 6)
    zero = jnp.zeros((nodes, cols), f32)
    attended, d_q, d_k, d_v = zero, zero, zero, zero
    for h in range(heads):
        mine = col_head == h
        q_h = jnp.where(mine, q2.astype(f32), 0.0).astype(bf16)
        a_h = jnp.where(mine, d_att.astype(f32), 0.0).astype(bf16)
        tanh2 = jnp.tanh(dot_t(q_h, k2) * (scale / cap_limit))
        weight2 = members[...] * jnp.exp(cap_limit * tanh2)
        prob2 = weight2 / jnp.sum(weight2, axis=1, keepdims=True)
        pb = prob2.astype(bf16)
        attended = jnp.where(mine, dot(pb, v2), attended)
        dprob = dot_t(a_h, v2)
        ds = prob2 * (dprob - jnp.sum(prob2 * dprob, axis=1, keepdims=True))
        dz = ds * (1.0 - tanh2 * tanh2) * scale
        d_q = jnp.where(mine, dot(dz.astype(bf16), k2), d_q)
        d_k = jnp.where(mine, dot(dz.T.astype(bf16), q2), d_k)
        d_v = jnp.where(mine, dot(prob2.T.astype(bf16), d_att), d_v)
    back = dot_t(d_q.astype(bf16), w_pqkv_ref[:, :cols])
    back = back + dot_t(d_k.astype(bf16), w_pqkv_ref[:, cols : 2 * cols])
    back = back + dot_t(d_v.astype(bf16), w_pqkv_ref[:, 2 * cols :])
    back_send[...] = back.astype(bf16)
    back_copies = [
        send_head(2, d, back_send.at[head_rows(head_peers[d])], back_recv.at[d])
        for d in range(n_head - 1)
    ]
    copies += back_copies
    out_send[...] = dot(attended.astype(bf16), w_po_ref[...]).astype(bf16)
    for c in back_copies:
        c.wait_recv()
    d_n = back_send[own_rows].astype(f32)
    for d in range(n_head - 1):
        d_n = d_n + back_recv[d].astype(f32)
    d_n = d_n - jnp.mean(d_n, axis=1, keepdims=True) - xhat * jnp.mean(d_n * xhat, axis=1, keepdims=True)
    d_hm[own_rows] = (cot_ref[own_rows].astype(f32) + inv * d_n).astype(bf16)
    d_hm_copies = [
        send_head(3, d, d_hm.at[own_rows], d_hm.at[own_rows]) for d in range(n_head - 1)
    ]
    out_copies = [
        send_head(4, d, out_send.at[head_rows(head_peers[d])], out_recv.at[d])
        for d in range(n_head - 1)
    ]
    copies += d_hm_copies + out_copies
    for c in d_hm_copies:
        c.wait_recv()

    d_mixed = dot_t(d_hm[...], w_o_ref[...]).astype(bf16)
    dm_f = d_mixed.astype(f32)
    dprob_s = head_sum(dm_f * v_f)

    def inners(s, total):
        dprob = head_sum(dot(hot[s], d_mixed) * kv[s][:, cols:].astype(f32))
        return total + dot_split(hot_t[s], prob_e[s] * dprob)

    inner = lax.fori_loop(0, n_grid, inners, prob_s * dprob_s)
    in_hi, in_lo = split(inner)

    def edge_grads(s, carry):
        h = hot[s]
        q_e = dot(h, query)
        dm_e = dot(h, d_mixed)
        dprob = head_sum(dm_e * kv[s][:, cols:].astype(f32))
        t = tanh_e[s]
        p = prob_e[s]
        dz = p * (dprob - (dot(h, in_hi) + dot(h, in_lo))) * (1.0 - t * t) * scale
        at = pl.ds(pl.multiple_of(s * cap, cap), cap)
        grads[at, :cols] = (dz * q_e).astype(bf16)
        grads[at, cols:] = (p.astype(bf16).astype(f32) * dm_e).astype(bf16)
        return carry

    lax.fori_loop(0, n_grid, edge_grads, 0)
    dz_s = prob_s * (dprob_s - inner) * (1.0 - tanh_s * tanh_s) * scale
    grads[n_grid * cap : n_grid * cap + nodes, :cols] = (dz_s * q_f).astype(bf16)
    grads[n_grid * cap : n_grid * cap + nodes, cols:] = (ps_b.astype(f32) * dm_f).astype(bf16)

    grad_copies = []
    for d in range(n_grid - 1):
        rows = grid_rows(grid_peers[d])
        grad_send[d] = dot(x_t[rows], grads[...]).astype(bf16)
        grad_copies.append(send_grid(1, d, grad_send.at[d], grad_recv.at[d]))
    copies += grad_copies
    grad_own = dot(x_t[grid_rows(my_grid)], grads[...])

    for c in out_copies:
        c.wait_recv()
    out_sum = out_send[own_rows].astype(f32)
    for d in range(n_head - 1):
        out_sum = out_sum + out_recv[d].astype(f32)
    hm_rows[...] = (hm1 + out_sum).astype(bf16)
    def head_cols(peer):
        return pl.ds(pl.multiple_of(peer * cols, cols), cols)

    col_copies = [
        send_head(5, d, hm_rows.at[:, head_cols(head_peers[d])], hm_cols.at[own_rows])
        for d in range(n_head - 1)
    ]
    copies += col_copies
    hm_cols[own_rows] = hm_rows[:, head_cols(my_head)]
    for c in col_copies:
        c.wait_recv()
    hm_ref[...] = hm_cols[...]

    for c in grad_copies:
        c.wait_recv()
    for d in range(n_grid - 1):
        grad_own = grad_own + grad_recv[d].astype(f32)
    grad_ref[...] = grad_own
    for c in copies:
        c.wait_send()


def body(
    grid_x, mesh_h, w_in, w_q, w_kv, w_o, w_pqkv, w_po, edge_src, edge_dst, edge_count, win_idx, cot
):
    n_grid = lax.axis_size("grid")
    n_head = lax.axis_size("head")
    cols = w_q.shape[1]
    nodes, width = mesh_h.shape
    cap = edge_src.shape[2]
    channels = grid_x.shape[1]
    own = nodes // n_head
    chunk = width // n_grid
    slots = n_grid * cap
    heads = cols // HEAD_SIZE
    pad = -channels % LANES
    gx = jnp.pad(grid_x.T, ((0, pad), (0, 0)))
    w_in_p = jnp.pad(w_in, ((0, pad), (0, 0)))
    live = lax.broadcasted_iota(jnp.int32, (n_grid, cap), 1) < edge_count[0][:, None]
    dst = jnp.where(live, edge_dst[0], -1).reshape(n_grid, 1, cap)
    src = edge_src[0].reshape(n_grid, 1, cap)
    vmem = pl.BlockSpec(memory_space=pltpu.VMEM)
    hm, grad = pl.pallas_call(
        functools.partial(kernel, n_grid, n_head),
        out_shape=(
            jax.ShapeDtypeStruct((nodes, cols), bf16),
            jax.ShapeDtypeStruct((chunk, 2 * cols), f32),
        ),
        in_specs=[vmem] * 12,
        out_specs=(vmem, vmem),
        scratch_shapes=[
            pltpu.VMEM((2 * n_grid - 1, channels + pad, cap), bf16),
            pltpu.VMEM((width, slots + nodes), bf16),
            pltpu.VMEM((n_grid, cap, nodes), bf16),
            pltpu.VMEM((n_grid, nodes, cap), bf16),
            pltpu.VMEM((n_grid, cap, 2 * cols), bf16),
            pltpu.VMEM((n_grid, cap, cols), f32),
            pltpu.VMEM((n_grid, cap, cols), f32),
            pltpu.VMEM((slots + nodes, 2 * cols), bf16),
            pltpu.VMEM((nodes, cols), bf16),
            pltpu.VMEM((nodes, 2 * cols), bf16),
            pltpu.VMEM((nodes, nodes), f32),
            pltpu.VMEM((nodes, width), bf16),
            pltpu.VMEM((n_head - 1, own, width), bf16),
            pltpu.VMEM((nodes, width), bf16),
            pltpu.VMEM((nodes, width), bf16),
            pltpu.VMEM((n_head - 1, own, width), bf16),
            pltpu.VMEM((own, width), bf16),
            pltpu.VMEM((nodes, cols), bf16),
            pltpu.VMEM((nodes, width), bf16),
            pltpu.VMEM((n_head - 1, own, width), bf16),
            pltpu.VMEM((nodes, width), bf16),
            pltpu.VMEM((n_grid - 1, chunk, 2 * cols), bf16),
            pltpu.VMEM((n_grid - 1, chunk, 2 * cols), bf16),
            pltpu.SemaphoreType.DMA((6, n_head - 1)),
            pltpu.SemaphoreType.DMA((6, n_head - 1)),
            pltpu.SemaphoreType.DMA((2, n_grid - 1)),
            pltpu.SemaphoreType.DMA((2, n_grid - 1)),
        ],
        compiler_params=pltpu.CompilerParams(
            collective_id=0, has_side_effects=True, vmem_limit_bytes=56 * 1024 * 1024
        ),
    )(
        gx,
        mesh_h,
        w_in_p,
        w_q,
        w_kv.reshape(width, 2 * cols),
        w_o,
        w_pqkv.reshape(width, 3 * cols),
        w_po,
        src,
        dst,
        win_idx,
        cot,
    )
    return hm, grad.reshape(chunk, 2, cols)


def solution(mesh):
    placed = (
        P(("groups", "grid"), None),
        P(("groups", "grid"), None),
        P(),
        P(None, "head"),
        P(None, None, "head"),
        P("head", None),
        P(None, None, "head"),
        P("head", None),
        P("grid", None, None),
        P("grid", None, None),
        P("grid", None),
        P("grid", None),
        P(("groups", "grid"), None),
    )
    return jax.shard_map(
        body,
        mesh=mesh,
        in_specs=placed,
        out_specs=(P(("groups", "grid"), "head"), P(("groups", "grid"), None, "head")),
        check_vma=False,
    )
```

```python
import functools
import math

import jax
import jax.numpy as jnp
from jax import lax
from jax.experimental import pallas as pl
from jax.experimental.pallas import tpu as pltpu
from jax.sharding import PartitionSpec as P

HEAD_SIZE = 64

norm_eps = 1e-05
cap_limit = 30.0
scale = 1.0 / math.sqrt(HEAD_SIZE)

f32 = jnp.float32
bf16 = jnp.bfloat16
MESH = pl.DeviceIdType.MESH


def normalize(values):
    row_mean = jnp.mean(values, axis=-1, keepdims=True)
    centred = values - row_mean
    var = jnp.mean(centred * centred, axis=-1, keepdims=True)
    inv = lax.rsqrt(var + norm_eps)
    return centred * inv, inv


def dot(a, b):
    return jnp.dot(a, b, preferred_element_type=f32)


def dot_t(a, b):
    return lax.dot_general(a, b, (((1,), (1,)), ((), ())), preferred_element_type=f32)


def t_dot(a, b):
    return lax.dot_general(a, b, (((0,), (0,)), ((), ())), preferred_element_type=f32)


def split(x):
    hi = x.astype(bf16)
    return hi, (x - hi.astype(f32)).astype(bf16)


def dot_split(a, x):
    hi, lo = split(x)
    return dot(a, hi) + dot(a, lo)


def kernel(
    n_grid,
    n_head,
    n_group,
    gx_ref,
    mesh_ref,
    w_in_ref,
    w_q_ref,
    w_kv_ref,
    w_o_ref,
    w_pqkv_ref,
    w_po_ref,
    src_ref,
    dst_ref,
    count_ref,
    win_ref,
    cot_ref,
    hm_ref,
    grad_ref,
    rows_t,
    x_t,
    hot,
    hot_t,
    kv,
    tanh_e,
    prob_e,
    grads,
    q_s,
    kv_s,
    members,
    w_in_p,
    dst_live,
    wo_full,
    mixed_full,
    hm1_s,
    out_send,
    out_recv,
    back_send,
    back_recv,
    dm_send,
    dm_full,
    pair_send,
    pair_recv,
    grad_send,
    grad_recv,
    hs_sem,
    hr_sem,
    gs_sem,
    gr_sem,
    ws_sem,
    wr_sem,
    xs_sem,
    xr_sem,
    cs_sem,
    cr_sem,
    ps_sem,
    pr_sem,
):
    width = mesh_ref.shape[1]
    nodes = mesh_ref.shape[0]
    cols = w_q_ref.shape[1]
    cap = src_ref.shape[2]
    channels = gx_ref.shape[0]
    padded = w_in_p.shape[0]
    heads = cols // HEAD_SIZE
    own = nodes // n_head
    chunk = width // n_grid
    my_grid = lax.axis_index("grid")
    my_head = lax.axis_index("head")
    my_group = lax.axis_index("groups")
    core = lax.rem(my_grid, 2)
    sibling = my_grid + 1 - 2 * core
    parts = 2 * n_group
    share = cols // parts
    n_pair = n_grid // 2
    my_pair = my_grid // 2
    grid_peers = [lax.rem(my_grid + d, n_grid) for d in range(1, n_grid)]
    head_peers = [lax.rem(my_head + d, n_head) for d in range(1, n_head)]
    head_from = [lax.rem(my_head + n_head - d, n_head) for d in range(1, n_head)]
    group_peers = [lax.rem(my_group + d, n_group) for d in range(1, n_group)]
    group_from = [lax.rem(my_group + n_group - d, n_group) for d in range(1, n_group)]
    pair_peers = [lax.rem(my_pair + d, n_pair) for d in range(1, n_pair)]

    barrier = pltpu.get_barrier_semaphore()
    for peer in grid_peers:
        pl.semaphore_signal(barrier, inc=1, device_id={"grid": peer}, device_id_type=MESH)
    for peer in head_peers:
        pl.semaphore_signal(barrier, inc=1, device_id={"head": peer}, device_id_type=MESH)

    for peer in group_peers:
        pl.semaphore_signal(barrier, inc=1, device_id={"groups": peer}, device_id_type=MESH)

    def send(src, dst, send_sem, recv_sem, to):
        c = pltpu.make_async_remote_copy(
            src_ref=src,
            dst_ref=dst,
            send_sem=send_sem,
            recv_sem=recv_sem,
            device_id=to,
            device_id_type=MESH,
        )
        c.start()
        return c

    def send_grid(phase, d, src, dst):
        to = {"grid": grid_peers[d]}
        return send(src, dst, gs_sem.at[phase, d], gr_sem.at[phase, d], to)

    def send_head(phase, d, src, dst):
        to = {"head": head_peers[d]}
        return send(src, dst, hs_sem.at[phase, d], hr_sem.at[phase, d], to)

    def head_rows(peer):
        return pl.ds(pl.multiple_of(peer * own, own), own)

    def grid_rows(peer):
        return pl.ds(pl.multiple_of(peer * chunk, chunk), chunk)

    def head_cols(peer):
        return pl.ds(pl.multiple_of(peer * cols, cols), cols)

    def wo_part(head, group, core):
        at = head * cols + (group * 2 + core) * share
        return pl.ds(pl.multiple_of(at, share), share)

    own_rows = head_rows(my_head)
    copies = []

    def gather_rows(slot, peer):
        idx = src_ref[0, pl.ds(peer, 1), :]
        total = None
        rows = gx_ref.shape[1]
        step = 512
        for start in range(0, rows, step):
            at = lax.broadcasted_iota(jnp.int32, (step, cap), 0) + start
            pick = jnp.where(at == idx, 1.0, 0.0).astype(bf16)
            part = dot(gx_ref[:, start : start + step], pick)
            total = part if total is None else total + part
        rows_t[slot, padded - 16 : padded] = jnp.zeros((16, cap), bf16)
        rows_t[slot, :channels] = total.astype(bf16)

    gather_rows(n_grid, grid_peers[0])
    pl.semaphore_wait(barrier, n_grid - 1 + n_head - 1 + n_group - 1)
    edge_copies = [send_grid(0, 0, rows_t.at[n_grid], rows_t.at[my_grid])]
    mine_q = pl.ds(pl.multiple_of((my_group * 2 + core) * share, share), share)
    wo_head = [
        send(
            w_o_ref.at[mine_q],
            wo_full.at[wo_part(my_head, my_group, core)],
            ws_sem.at[d],
            wr_sem.at[d],
            {"head": head_peers[d]},
        )
        for d in range(n_head - 1)
    ]
    for d in range(1, n_grid - 1):
        gather_rows(n_grid + d, grid_peers[d])
        edge_copies.append(send_grid(0, d, rows_t.at[n_grid + d], rows_t.at[my_grid]))
    gather_rows(my_grid, my_grid)
    copies += edge_copies + wo_head
    wo_full[head_cols(my_head)] = w_o_ref[...]
    w_in_p[padded - 16 : padded] = jnp.zeros((16, width), bf16)
    w_in_p[:channels] = w_in_ref[...]
    same = lax.broadcasted_iota(jnp.int32, (n_grid, n_grid), 0) == lax.broadcasted_iota(
        jnp.int32, (n_grid, n_grid), 1
    )
    counts = jnp.sum(jnp.where(same, count_ref[...], 0).astype(f32), axis=1, keepdims=True)
    slot_at = lax.broadcasted_iota(jnp.int32, (n_grid, cap), 1).astype(f32)
    dst_live[...] = jnp.where(slot_at < counts, dst_ref[0], -1)

    mesh_f = mesh_ref[...].astype(f32)
    mesh_n = normalize(mesh_f)[0]
    x_t[:, n_grid * cap : n_grid * cap + nodes] = mesh_n.T.astype(bf16)
    mesh_n = mesh_n.astype(bf16)
    q_s[...] = dot(mesh_n, w_q_ref[...]).astype(bf16)
    kv_s[...] = dot(mesh_n, w_kv_ref[...]).astype(bf16)

    def onehots(s, carry):
        at = lax.broadcasted_iota(jnp.int32, (nodes, cap), 0)
        pick = jnp.where(at == dst_live[pl.ds(s, 1), :], 1.0, 0.0)
        hot_t[s] = pick.astype(bf16)
        hot[s] = pick.T.astype(bf16)
        return carry

    lax.fori_loop(0, n_grid, onehots, 0)

    row_at = lax.shift_right_logical(lax.broadcasted_iota(jnp.int32, (cols, cols), 0), 6)
    col_at = lax.shift_right_logical(lax.broadcasted_iota(jnp.int32, (cols, cols), 1), 6)
    same_head = jnp.where(row_at == col_at, 1.0, 0.0).astype(bf16)

    def head_sum(x):
        hi, lo = split(x)
        return dot(hi, same_head) + dot(lo, same_head)

    for c in edge_copies:
        c.wait_recv()

    def embed(s, carry):
        row = normalize(t_dot(rows_t[s], w_in_p[...]))[0]
        x_t[:, pl.ds(pl.multiple_of(s * cap, cap), cap)] = row.T.astype(bf16)
        kv[s] = dot(row.astype(bf16), w_kv_ref[...]).astype(bf16)
        return carry

    lax.fori_loop(0, n_grid, embed, 0)

    wo_group, wo_core = [], []
    for d in range(n_head - 1):
        wo_head[d].wait_recv()
        at = wo_part(head_from[d], my_group, core)
        for g in range(n_group - 1):
            to = {"groups": group_peers[g]}
            part = wo_full.at[at]
            wo_group.append(send(part, part, xs_sem.at[g, d], xr_sem.at[g, d], to))
        part = wo_full.at[at]
        wo_core.append(send(part, part, cs_sem.at[0, d], cr_sem.at[0, d], {"grid": sibling}))

    query = q_s[...]
    q_f = query.astype(f32)
    k_f = kv_s[:, :cols].astype(f32)
    v_f = kv_s[:, cols:].astype(f32)
    tanh_s = jnp.tanh(head_sum(q_f * k_f) * (scale / cap_limit))
    weight_s = jnp.exp(cap_limit * tanh_s)

    def scores(s, denom):
        q_e = dot(hot[s], query)
        t = jnp.tanh(head_sum(q_e * kv[s][:, :cols].astype(f32)) * (scale / cap_limit))
        w = jnp.exp(cap_limit * t)
        tanh_e[s] = t
        prob_e[s] = w
        return denom + dot_split(hot_t[s], w)

    denom = lax.fori_loop(0, n_grid, scores, weight_s)
    recip = 1.0 / denom
    prob_s = weight_s * recip
    recip_hi, recip_lo = split(recip)
    ps_b = prob_s.astype(bf16)

    def mix(s, total):
        p = prob_e[s] * (dot(hot[s], recip_hi) + dot(hot[s], recip_lo))
        prob_e[s] = p
        v = kv[s][:, cols:].astype(f32)
        return total + dot_split(hot_t[s], p.astype(bf16).astype(f32) * v)

    mixed = lax.fori_loop(0, n_grid, mix, ps_b.astype(f32) * v_f).astype(bf16)
    mixed_full[my_head] = mixed
    mix_copies = [
        send_head(0, d, mixed_full.at[my_head], mixed_full.at[my_head])
        for d in range(n_head - 1)
    ]

    node = lax.broadcasted_iota(jnp.int32, (nodes, nodes), 0)
    win = win_ref[...]
    count = jnp.zeros((nodes, nodes), f32)
    for m in range(win.shape[0]):
        count = count + jnp.where(node == win[m : m + 1, :], 1.0, 0.0)
    members[...] = count.T
    d_att = dot_t(cot_ref[...], w_po_ref[...]).astype(bf16)

    for g in range(n_group - 1):
        for d in range(n_head - 1):
            wo_group[d * (n_group - 1) + g].wait_recv()
            part = wo_full.at[wo_part(head_from[d], group_from[g], core)]
            to = {"grid": sibling}
            wo_core.append(send(part, part, cs_sem.at[g + 1, d], cr_sem.at[g + 1, d], to))
    copies += wo_group + wo_core + mix_copies

    def enc_term(head):
        return dot(mixed_full[head], wo_full[head_cols(head)]).astype(bf16).astype(f32)

    hm1 = mesh_f + enc_term(my_head)
    for c in wo_core:
        c.wait_recv()
    for d in range(n_head - 1):
        mix_copies[d].wait_recv()
        hm1 = hm1 + enc_term(head_from[d])
    hm1_s[...] = hm1
    normed = normalize(hm1)[0].astype(bf16)

    q2, k2, v2 = [dot(normed, w_pqkv_ref[t]).astype(bf16) for t in range(3)]
    col_head = lax.shift_right_logical(lax.broadcasted_iota(jnp.int32, (nodes, cols), 1), 6)
    zero = jnp.zeros((nodes, cols), f32)
    attended, d_q, d_k, d_v = zero, zero, zero, zero
    for h in range(heads):
        mine = col_head == h
        q_h = jnp.where(mine, q2.astype(f32), 0.0).astype(bf16)
        a_h = jnp.where(mine, d_att.astype(f32), 0.0).astype(bf16)
        tanh2 = jnp.tanh(dot_t(q_h, k2) * (scale / cap_limit))
        weight2 = members[...] * jnp.exp(cap_limit * tanh2)
        prob2 = weight2 / jnp.sum(weight2, axis=1, keepdims=True)
        pb = prob2.astype(bf16)
        attended = jnp.where(mine, dot(pb, v2), attended)
        dprob = dot_t(a_h, v2)
        ds = prob2 * (dprob - jnp.sum(prob2 * dprob, axis=1, keepdims=True))
        dz = ds * (1.0 - tanh2 * tanh2) * scale
        d_q = jnp.where(mine, dot(dz.astype(bf16), k2), d_q)
        d_k = jnp.where(mine, dot(dz.T.astype(bf16), q2), d_k)
        d_v = jnp.where(mine, dot(prob2.T.astype(bf16), d_att), d_v)
    back = dot_t(d_q.astype(bf16), w_pqkv_ref[0])
    back = back + dot_t(d_k.astype(bf16), w_pqkv_ref[1])
    back = back + dot_t(d_v.astype(bf16), w_pqkv_ref[2])
    back_send[...] = back.astype(bf16)
    back_copies = [
        send_head(1, d, back_send.at[head_rows(head_peers[d])], back_recv.at[d])
        for d in range(n_head - 1)
    ]
    copies += back_copies
    attended = attended.astype(bf16)
    for h in range(n_head):
        out_send[h] = dot(attended, w_po_ref[:, h * cols : (h + 1) * cols]).astype(bf16)
    xhat, inv = normalize(hm1_s[own_rows])
    for c in back_copies:
        c.wait_recv()
    d_n = back_send[own_rows].astype(f32)
    for d in range(n_head - 1):
        d_n = d_n + back_recv[d].astype(f32)
    d_n = d_n - jnp.mean(d_n, axis=1, keepdims=True) - xhat * jnp.mean(d_n * xhat, axis=1, keepdims=True)
    d_hm = (cot_ref[own_rows].astype(f32) + inv * d_n).astype(bf16)
    dm_rows = dot_t(d_hm, wo_full[...]).astype(bf16)
    for h in range(n_head):
        dm_send[h] = dm_rows[:, h * cols : (h + 1) * cols]
    dm_copies = [
        send_head(2, d, dm_send.at[head_peers[d]], dm_full.at[own_rows]) for d in range(n_head - 1)
    ]
    dm_full[own_rows] = dm_send[my_head]
    out_copies = [
        send_head(3, d, out_send.at[head_peers[d]], out_recv.at[d]) for d in range(n_head - 1)
    ]
    copies += dm_copies + out_copies
    for c in dm_copies:
        c.wait_recv()

    d_mixed = dm_full[...]
    dm_f = d_mixed.astype(f32)
    dprob_s = head_sum(dm_f * v_f)

    def inners(s, total):
        dprob = head_sum(dot(hot[s], d_mixed) * kv[s][:, cols:].astype(f32))
        return total + dot_split(hot_t[s], prob_e[s] * dprob)

    inner = lax.fori_loop(0, n_grid, inners, prob_s * dprob_s)
    in_hi, in_lo = split(inner)

    def edge_grads(s, carry):
        h = hot[s]
        q_e = dot(h, query)
        dm_e = dot(h, d_mixed)
        dprob = head_sum(dm_e * kv[s][:, cols:].astype(f32))
        t = tanh_e[s]
        p = prob_e[s]
        dz = p * (dprob - (dot(h, in_hi) + dot(h, in_lo))) * (1.0 - t * t) * scale
        at = pl.ds(pl.multiple_of(s * cap, cap), cap)
        grads[at, :cols] = (dz * q_e).astype(bf16)
        grads[at, cols:] = (p.astype(bf16).astype(f32) * dm_e).astype(bf16)
        return carry

    lax.fori_loop(0, n_grid, edge_grads, 0)
    dz_s = prob_s * (dprob_s - inner) * (1.0 - tanh_s * tanh_s) * scale
    grads[n_grid * cap : n_grid * cap + nodes, :cols] = (dz_s * q_f).astype(bf16)
    grads[n_grid * cap : n_grid * cap + nodes, cols:] = (ps_b.astype(f32) * dm_f).astype(bf16)

    def grad_term(pair, of_core):
        return dot(x_t[grid_rows(pair * 2 + of_core)], grads[...])

    pair_copies = []
    for j in range(n_pair):
        to_pair = pair_peers[j] if j < n_pair - 1 else my_pair
        pair_send[j] = grad_term(to_pair, 1 - core).astype(bf16)
        pair_copies.append(
            send(
                pair_send.at[j], pair_recv.at[j], ps_sem.at[j], pr_sem.at[j], {"grid": sibling}
            )
        )
    grad_copies = []
    for j in range(n_pair - 1):
        term = grad_term(pair_peers[j], core)
        pair_copies[j].wait_recv()
        grad_send[j] = (term + pair_recv[j].astype(f32)).astype(bf16)
        to = {"grid": pair_peers[j] * 2 + core}
        grad_copies.append(send(grad_send.at[j], grad_recv.at[j], gs_sem.at[1, j], gr_sem.at[1, j], to))
    copies += pair_copies + grad_copies
    grad_own = grad_term(my_pair, core)
    pair_copies[n_pair - 1].wait_recv()
    grad_own = grad_own + pair_recv[n_pair - 1].astype(f32)

    out_sum = out_send[my_head].astype(f32)
    for d in range(n_head - 1):
        out_copies[d].wait_recv()
        out_sum = out_sum + out_recv[d].astype(f32)
    hm_ref[...] = hm1_s[:, head_cols(my_head)] + out_sum

    for j in range(n_pair - 1):
        grad_copies[j].wait_recv()
        grad_own = grad_own + grad_recv[j].astype(f32)
    grad_ref[...] = grad_own
    for c in copies:
        c.wait_send()


def body(
    grid_x, mesh_h, w_in, w_q, w_kv, w_o, w_pqkv, w_po, edge_src, edge_dst, edge_count, win_idx, cot
):
    n_grid = lax.axis_size("grid")
    n_head = lax.axis_size("head")
    n_group = lax.axis_size("groups")
    cols = w_q.shape[1]
    nodes, width = mesh_h.shape
    cap = edge_src.shape[2]
    channels = grid_x.shape[1]
    own = nodes // n_head
    chunk = width // n_grid
    slots = n_grid * cap
    padded = channels + (-channels % 16)
    vmem = pl.BlockSpec(memory_space=pltpu.VMEM)
    hm, grad = pl.pallas_call(
        functools.partial(kernel, n_grid, n_head, n_group),
        out_shape=(
            jax.ShapeDtypeStruct((nodes, cols), f32),
            jax.ShapeDtypeStruct((chunk, 2 * cols), f32),
        ),
        in_specs=[vmem] * 13,
        out_specs=(vmem, vmem),
        scratch_shapes=[
            pltpu.VMEM((2 * n_grid - 1, padded, cap), bf16),
            pltpu.VMEM((width, slots + nodes), bf16),
            pltpu.VMEM((n_grid, cap, nodes), bf16),
            pltpu.VMEM((n_grid, nodes, cap), bf16),
            pltpu.VMEM((n_grid, cap, 2 * cols), bf16),
            pltpu.VMEM((n_grid, cap, cols), f32),
            pltpu.VMEM((n_grid, cap, cols), f32),
            pltpu.VMEM((slots + nodes, 2 * cols), bf16),
            pltpu.VMEM((nodes, cols), bf16),
            pltpu.VMEM((nodes, 2 * cols), bf16),
            pltpu.VMEM((nodes, nodes), f32),
            pltpu.VMEM((padded, width), bf16),
            pltpu.VMEM((n_grid, cap), jnp.int32),
            pltpu.VMEM((n_head * cols, width), bf16),
            pltpu.VMEM((n_head, nodes, cols), bf16),
            pltpu.VMEM((nodes, width), f32),
            pltpu.VMEM((n_head, nodes, cols), bf16),
            pltpu.VMEM((n_head - 1, nodes, cols), bf16),
            pltpu.VMEM((nodes, width), bf16),
            pltpu.VMEM((n_head - 1, own, width), bf16),
            pltpu.VMEM((n_head, own, cols), bf16),
            pltpu.VMEM((nodes, cols), bf16),
            pltpu.VMEM((n_grid // 2, chunk, 2 * cols), bf16),
            pltpu.VMEM((n_grid // 2, chunk, 2 * cols), bf16),
            pltpu.VMEM((n_grid // 2 - 1, chunk, 2 * cols), bf16),
            pltpu.VMEM((n_grid // 2 - 1, chunk, 2 * cols), bf16),
            pltpu.SemaphoreType.DMA((4, n_head - 1)),
            pltpu.SemaphoreType.DMA((4, n_head - 1)),
            pltpu.SemaphoreType.DMA((2, n_grid - 1)),
            pltpu.SemaphoreType.DMA((2, n_grid - 1)),
            pltpu.SemaphoreType.DMA((n_head - 1,)),
            pltpu.SemaphoreType.DMA((n_head - 1,)),
            pltpu.SemaphoreType.DMA((n_group - 1, n_head - 1)),
            pltpu.SemaphoreType.DMA((n_group - 1, n_head - 1)),
            pltpu.SemaphoreType.DMA((n_group, n_head - 1)),
            pltpu.SemaphoreType.DMA((n_group, n_head - 1)),
            pltpu.SemaphoreType.DMA((n_grid // 2,)),
            pltpu.SemaphoreType.DMA((n_grid // 2,)),
        ],
        compiler_params=pltpu.CompilerParams(
            collective_id=0, has_side_effects=True, vmem_limit_bytes=56 * 1024 * 1024
        ),
    )(
        grid_x.T,
        mesh_h,
        w_in,
        w_q,
        w_kv.reshape(width, 2 * cols),
        w_o,
        w_pqkv.transpose(1, 0, 2),
        w_po,
        edge_src,
        edge_dst,
        edge_count,
        win_idx.T,
        cot,
    )
    return hm.astype(bf16), grad.reshape(chunk, 2, cols)


def solution(mesh):
    placed = (
        P(("groups", "grid"), None),
        P(("groups", "grid"), None),
        P(),
        P(None, "head"),
        P(None, None, "head"),
        P("head", None),
        P(None, None, "head"),
        P("head", None),
        P("grid", None, None),
        P("grid", None, None),
        P("grid", None),
        P("grid", None),
        P(("groups", "grid"), None),
    )
    return jax.shard_map(
        body,
        mesh=mesh,
        in_specs=placed,
        out_specs=(P(("groups", "grid"), "head"), P(("groups", "grid"), None, "head")),
        check_vma=False,
    )
```

```python
import functools
import math

import jax
import jax.numpy as jnp
from jax import lax
from jax.experimental import pallas as pl
from jax.experimental.pallas import tpu as pltpu
from jax.sharding import PartitionSpec as P

HEAD_SIZE = 64

norm_eps = 1e-05
cap_limit = 30.0
scale = 1.0 / math.sqrt(HEAD_SIZE)

f32 = jnp.float32
bf16 = jnp.bfloat16
MESH = pl.DeviceIdType.MESH


def normalize(values):
    row_mean = jnp.mean(values, axis=-1, keepdims=True)
    centred = values - row_mean
    var = jnp.mean(centred * centred, axis=-1, keepdims=True)
    inv = lax.rsqrt(var + norm_eps)
    return centred * inv, inv


def dot(a, b):
    return jnp.dot(a, b, preferred_element_type=f32)


def dot_t(a, b):
    return lax.dot_general(a, b, (((1,), (1,)), ((), ())), preferred_element_type=f32)


def t_dot(a, b):
    return lax.dot_general(a, b, (((0,), (0,)), ((), ())), preferred_element_type=f32)


def split(x):
    hi = x.astype(bf16)
    return hi, (x - hi.astype(f32)).astype(bf16)


def dot_split(a, x):
    hi, lo = split(x)
    return dot(a, hi) + dot(a, lo)


def kernel(
    n_grid,
    n_head,
    n_group,
    gx_ref,
    mesh_ref,
    w_in_ref,
    w_q_ref,
    w_kv_ref,
    w_o_ref,
    w_pqkv_ref,
    w_po_ref,
    src_ref,
    dst_ref,
    count_ref,
    win_ref,
    cot_ref,
    hm_ref,
    grad_ref,
    rows_t,
    x_t,
    hot,
    hot_t,
    kv,
    tanh_e,
    prob_e,
    grads,
    q_s,
    kv_s,
    members,
    w_kv2,
    w_in_p,
    dst_live,
    wo_full,
    mixed_full,
    hm1_s,
    out_send,
    out_recv,
    back_send,
    back_recv,
    dm_send,
    dm_full,
    pair_send,
    pair_recv,
    grad_send,
    grad_recv,
    hs_sem,
    hr_sem,
    gs_sem,
    gr_sem,
    ws_sem,
    wr_sem,
    xs_sem,
    xr_sem,
    cs_sem,
    cr_sem,
    ps_sem,
    pr_sem,
):
    width = mesh_ref.shape[1]
    nodes = mesh_ref.shape[0]
    cols = w_q_ref.shape[1]
    cap = src_ref.shape[2]
    channels = gx_ref.shape[0]
    padded = w_in_p.shape[0]
    heads = cols // HEAD_SIZE
    own = nodes // n_head
    chunk = width // n_grid
    my_grid = lax.axis_index("grid")
    my_head = lax.axis_index("head")
    my_group = lax.axis_index("groups")
    core = lax.rem(my_grid, 2)
    sibling = my_grid + 1 - 2 * core
    parts = 2 * n_group
    share = cols // parts
    n_pair = n_grid // 2
    my_pair = my_grid // 2
    grid_peers = [lax.rem(my_grid + d, n_grid) for d in range(1, n_grid)]
    head_peers = [lax.rem(my_head + d, n_head) for d in range(1, n_head)]
    head_from = [lax.rem(my_head + n_head - d, n_head) for d in range(1, n_head)]
    group_peers = [lax.rem(my_group + d, n_group) for d in range(1, n_group)]
    group_from = [lax.rem(my_group + n_group - d, n_group) for d in range(1, n_group)]
    pair_peers = [lax.rem(my_pair + d, n_pair) for d in range(1, n_pair)]

    barrier = pltpu.get_barrier_semaphore()
    for peer in grid_peers:
        pl.semaphore_signal(barrier, inc=1, device_id={"grid": peer}, device_id_type=MESH)
    for peer in head_peers:
        pl.semaphore_signal(barrier, inc=1, device_id={"head": peer}, device_id_type=MESH)

    for peer in group_peers:
        pl.semaphore_signal(barrier, inc=1, device_id={"groups": peer}, device_id_type=MESH)

    def send(src, dst, send_sem, recv_sem, to):
        c = pltpu.make_async_remote_copy(
            src_ref=src,
            dst_ref=dst,
            send_sem=send_sem,
            recv_sem=recv_sem,
            device_id=to,
            device_id_type=MESH,
        )
        c.start()
        return c

    def send_grid(phase, d, src, dst):
        to = {"grid": grid_peers[d]}
        return send(src, dst, gs_sem.at[phase, d], gr_sem.at[phase, d], to)

    def send_head(phase, d, src, dst):
        to = {"head": head_peers[d]}
        return send(src, dst, hs_sem.at[phase, d], hr_sem.at[phase, d], to)

    def head_rows(peer):
        return pl.ds(pl.multiple_of(peer * own, own), own)

    def grid_rows(peer):
        return pl.ds(pl.multiple_of(peer * chunk, chunk), chunk)

    def head_cols(peer):
        return pl.ds(pl.multiple_of(peer * cols, cols), cols)

    def wo_part(head, group, core):
        at = head * cols + (group * 2 + core) * share
        return pl.ds(pl.multiple_of(at, share), share)

    own_rows = head_rows(my_head)
    copies = []

    def gather_rows(slot, peer):
        idx = src_ref[0, pl.ds(peer, 1), :]
        total = None
        rows = gx_ref.shape[1]
        step = 512
        for start in range(0, rows, step):
            at = lax.broadcasted_iota(jnp.int32, (step, cap), 0) + start
            pick = jnp.where(at == idx, 1.0, 0.0).astype(bf16)
            part = dot(gx_ref[:, start : start + step], pick)
            total = part if total is None else total + part
        rows_t[slot, padded - 16 : padded] = jnp.zeros((16, cap), bf16)
        rows_t[slot, :channels] = total.astype(bf16)

    gather_rows(n_grid, grid_peers[0])
    pl.semaphore_wait(barrier, n_grid - 1 + n_head - 1 + n_group - 1)
    edge_copies = [send_grid(0, 0, rows_t.at[n_grid], rows_t.at[my_grid])]
    mine_q = pl.ds(pl.multiple_of((my_group * 2 + core) * share, share), share)
    wo_head = [
        send(
            w_o_ref.at[mine_q],
            wo_full.at[wo_part(my_head, my_group, core)],
            ws_sem.at[d],
            wr_sem.at[d],
            {"head": head_peers[d]},
        )
        for d in range(n_head - 1)
    ]
    for d in range(1, n_grid - 1):
        gather_rows(n_grid + d, grid_peers[d])
        edge_copies.append(send_grid(0, d, rows_t.at[n_grid + d], rows_t.at[my_grid]))
    gather_rows(my_grid, my_grid)
    copies += edge_copies + wo_head
    wo_full[head_cols(my_head)] = w_o_ref[...]
    w_in_p[padded - 16 : padded] = jnp.zeros((16, width), bf16)
    w_in_p[:channels] = w_in_ref[...]
    for t in range(2):
        w_kv2[:, t * cols : (t + 1) * cols] = w_kv_ref[:, t, :]
    same = lax.broadcasted_iota(jnp.int32, (n_grid, n_grid), 0) == lax.broadcasted_iota(
        jnp.int32, (n_grid, n_grid), 1
    )
    counts = jnp.sum(jnp.where(same, count_ref[...], 0).astype(f32), axis=1, keepdims=True)
    slot_at = lax.broadcasted_iota(jnp.int32, (n_grid, cap), 1).astype(f32)
    dst_live[...] = jnp.where(slot_at < counts, dst_ref[0], -1)

    mesh_f = mesh_ref[...].astype(f32)
    mesh_n = normalize(mesh_f)[0]
    x_t[:, n_grid * cap : n_grid * cap + nodes] = mesh_n.T.astype(bf16)
    mesh_n = mesh_n.astype(bf16)
    q_s[...] = dot(mesh_n, w_q_ref[...]).astype(bf16)
    kv_s[...] = dot(mesh_n, w_kv2[...]).astype(bf16)

    def onehots(s, carry):
        at = lax.broadcasted_iota(jnp.int32, (nodes, cap), 0)
        pick = jnp.where(at == dst_live[pl.ds(s, 1), :], 1.0, 0.0)
        hot_t[s] = pick.astype(bf16)
        hot[s] = pick.T.astype(bf16)
        return carry

    lax.fori_loop(0, n_grid, onehots, 0)

    row_at = lax.shift_right_logical(lax.broadcasted_iota(jnp.int32, (cols, cols), 0), 6)
    col_at = lax.shift_right_logical(lax.broadcasted_iota(jnp.int32, (cols, cols), 1), 6)
    same_head = jnp.where(row_at == col_at, 1.0, 0.0).astype(bf16)

    def head_sum(x):
        hi, lo = split(x)
        return dot(hi, same_head) + dot(lo, same_head)

    for c in edge_copies:
        c.wait_recv()

    def embed(s, carry):
        row = normalize(t_dot(rows_t[s], w_in_p[...]))[0]
        x_t[:, pl.ds(pl.multiple_of(s * cap, cap), cap)] = row.T.astype(bf16)
        kv[s] = dot(row.astype(bf16), w_kv2[...]).astype(bf16)
        return carry

    lax.fori_loop(0, n_grid, embed, 0)

    query = q_s[...]
    q_f = query.astype(f32)
    k_f = kv_s[:, :cols].astype(f32)
    v_f = kv_s[:, cols:].astype(f32)
    tanh_s = jnp.tanh(head_sum(q_f * k_f) * (scale / cap_limit))
    weight_s = jnp.exp(cap_limit * tanh_s)

    def scores(s, denom):
        q_e = dot(hot[s], query)
        t = jnp.tanh(head_sum(q_e * kv[s][:, :cols].astype(f32)) * (scale / cap_limit))
        w = jnp.exp(cap_limit * t)
        tanh_e[s] = t
        prob_e[s] = w
        return denom + dot_split(hot_t[s], w)

    denom = lax.fori_loop(0, n_grid, scores, weight_s)
    wo_group, wo_core = [], []
    for d in range(n_head - 1):
        wo_head[d].wait_recv()
        at = wo_part(head_from[d], my_group, core)
        for g in range(n_group - 1):
            to = {"groups": group_peers[g]}
            part = wo_full.at[at]
            wo_group.append(send(part, part, xs_sem.at[g, d], xr_sem.at[g, d], to))
        part = wo_full.at[at]
        wo_core.append(send(part, part, cs_sem.at[0, d], cr_sem.at[0, d], {"grid": sibling}))

    recip = 1.0 / denom
    prob_s = weight_s * recip
    recip_hi, recip_lo = split(recip)
    ps_b = prob_s.astype(bf16)

    def mix(s, total):
        p = prob_e[s] * (dot(hot[s], recip_hi) + dot(hot[s], recip_lo))
        prob_e[s] = p
        v = kv[s][:, cols:].astype(f32)
        return total + dot_split(hot_t[s], p.astype(bf16).astype(f32) * v)

    mixed = lax.fori_loop(0, n_grid, mix, ps_b.astype(f32) * v_f).astype(bf16)
    mixed_full[my_head] = mixed
    mix_copies = [
        send_head(0, d, mixed_full.at[my_head], mixed_full.at[my_head])
        for d in range(n_head - 1)
    ]

    node = lax.broadcasted_iota(jnp.int32, (nodes, nodes), 0)
    win = win_ref[...]
    count = jnp.zeros((nodes, nodes), f32)
    for m in range(win.shape[0]):
        count = count + jnp.where(node == win[m : m + 1, :], 1.0, 0.0)
    members[...] = count.T
    d_att = dot_t(cot_ref[...], w_po_ref[...]).astype(bf16)

    for g in range(n_group - 1):
        for d in range(n_head - 1):
            wo_group[d * (n_group - 1) + g].wait_recv()
            part = wo_full.at[wo_part(head_from[d], group_from[g], core)]
            to = {"grid": sibling}
            wo_core.append(send(part, part, cs_sem.at[g + 1, d], cr_sem.at[g + 1, d], to))
    copies += wo_group + wo_core + mix_copies

    def enc_term(head):
        return dot(mixed_full[head], wo_full[head_cols(head)]).astype(bf16).astype(f32)

    hm1 = mesh_f + enc_term(my_head)
    for c in wo_core:
        c.wait_recv()
    for d in range(n_head - 1):
        mix_copies[d].wait_recv()
        hm1 = hm1 + enc_term(head_from[d])
    hm1_s[...] = hm1
    normed = normalize(hm1)[0].astype(bf16)

    q2, k2, v2 = [dot(normed, w_pqkv_ref[t]).astype(bf16) for t in range(3)]
    col_head = lax.shift_right_logical(lax.broadcasted_iota(jnp.int32, (nodes, cols), 1), 6)
    zero = jnp.zeros((nodes, cols), f32)
    attended, d_q, d_k, d_v = zero, zero, zero, zero
    for h in range(heads):
        mine = col_head == h
        q_h = jnp.where(mine, q2.astype(f32), 0.0).astype(bf16)
        a_h = jnp.where(mine, d_att.astype(f32), 0.0).astype(bf16)
        tanh2 = jnp.tanh(dot_t(q_h, k2) * (scale / cap_limit))
        weight2 = members[...] * jnp.exp(cap_limit * tanh2)
        prob2 = weight2 / jnp.sum(weight2, axis=1, keepdims=True)
        pb = prob2.astype(bf16)
        attended = jnp.where(mine, dot(pb, v2), attended)
        dprob = dot_t(a_h, v2)
        ds = prob2 * (dprob - jnp.sum(prob2 * dprob, axis=1, keepdims=True))
        dz = ds * (1.0 - tanh2 * tanh2) * scale
        d_q = jnp.where(mine, dot(dz.astype(bf16), k2), d_q)
        d_k = jnp.where(mine, dot(dz.T.astype(bf16), q2), d_k)
        d_v = jnp.where(mine, dot(prob2.T.astype(bf16), d_att), d_v)
    back = dot_t(d_q.astype(bf16), w_pqkv_ref[0])
    back = back + dot_t(d_k.astype(bf16), w_pqkv_ref[1])
    back = back + dot_t(d_v.astype(bf16), w_pqkv_ref[2])
    back_send[...] = back.astype(bf16)
    back_copies = [
        send_head(1, d, back_send.at[head_rows(head_peers[d])], back_recv.at[d])
        for d in range(n_head - 1)
    ]
    copies += back_copies
    attended = attended.astype(bf16)
    for h in range(n_head):
        out_send[h] = dot(attended, w_po_ref[:, h * cols : (h + 1) * cols]).astype(bf16)
    xhat, inv = normalize(hm1_s[own_rows])
    for c in back_copies:
        c.wait_recv()
    d_n = back_send[own_rows].astype(f32)
    for d in range(n_head - 1):
        d_n = d_n + back_recv[d].astype(f32)
    d_n = d_n - jnp.mean(d_n, axis=1, keepdims=True) - xhat * jnp.mean(d_n * xhat, axis=1, keepdims=True)
    d_hm = (cot_ref[own_rows].astype(f32) + inv * d_n).astype(bf16)
    dm_rows = dot_t(d_hm, wo_full[...]).astype(bf16)
    for h in range(n_head):
        dm_send[h] = dm_rows[:, h * cols : (h + 1) * cols]
    dm_copies = [
        send_head(2, d, dm_send.at[head_peers[d]], dm_full.at[own_rows]) for d in range(n_head - 1)
    ]
    dm_full[own_rows] = dm_send[my_head]
    for c in dm_copies:
        c.wait_recv()
    out_copies = [
        send_head(3, d, out_send.at[head_peers[d]], out_recv.at[d]) for d in range(n_head - 1)
    ]
    copies += dm_copies + out_copies

    d_mixed = dm_full[...]
    dm_f = d_mixed.astype(f32)
    dprob_s = head_sum(dm_f * v_f)

    def inners(s, total):
        dprob = head_sum(dot(hot[s], d_mixed) * kv[s][:, cols:].astype(f32))
        return total + dot_split(hot_t[s], prob_e[s] * dprob)

    inner = lax.fori_loop(0, n_grid, inners, prob_s * dprob_s)
    in_hi, in_lo = split(inner)

    def edge_grads(s, carry):
        h = hot[s]
        q_e = dot(h, query)
        dm_e = dot(h, d_mixed)
        dprob = head_sum(dm_e * kv[s][:, cols:].astype(f32))
        t = tanh_e[s]
        p = prob_e[s]
        dz = p * (dprob - (dot(h, in_hi) + dot(h, in_lo))) * (1.0 - t * t) * scale
        at = pl.ds(pl.multiple_of(s * cap, cap), cap)
        grads[at, :cols] = (dz * q_e).astype(bf16)
        grads[at, cols:] = (p.astype(bf16).astype(f32) * dm_e).astype(bf16)
        return carry

    lax.fori_loop(0, n_grid, edge_grads, 0)
    dz_s = prob_s * (dprob_s - inner) * (1.0 - tanh_s * tanh_s) * scale
    grads[n_grid * cap : n_grid * cap + nodes, :cols] = (dz_s * q_f).astype(bf16)
    grads[n_grid * cap : n_grid * cap + nodes, cols:] = (ps_b.astype(f32) * dm_f).astype(bf16)

    def grad_term(pair, of_core):
        return dot(x_t[grid_rows(pair * 2 + of_core)], grads[...])

    pair_copies = []
    for j in range(n_pair):
        to_pair = pair_peers[j] if j < n_pair - 1 else my_pair
        pair_send[j] = grad_term(to_pair, 1 - core).astype(bf16)
        pair_copies.append(
            send(
                pair_send.at[j], pair_recv.at[j], ps_sem.at[j], pr_sem.at[j], {"grid": sibling}
            )
        )
    grad_copies = []
    for j in range(n_pair - 1):
        term = grad_term(pair_peers[j], core)
        pair_copies[j].wait_recv()
        grad_send[j] = (term + pair_recv[j].astype(f32)).astype(bf16)
        to = {"grid": pair_peers[j] * 2 + core}
        grad_copies.append(send(grad_send.at[j], grad_recv.at[j], gs_sem.at[1, j], gr_sem.at[1, j], to))
    copies += pair_copies + grad_copies
    grad_own = grad_term(my_pair, core)
    pair_copies[n_pair - 1].wait_recv()
    grad_own = grad_own + pair_recv[n_pair - 1].astype(f32)

    out_sum = out_send[my_head].astype(f32)
    for d in range(n_head - 1):
        out_copies[d].wait_recv()
        out_sum = out_sum + out_recv[d].astype(f32)
    hm_ref[...] = hm1_s[:, head_cols(my_head)] + out_sum

    for j in range(n_pair - 1):
        grad_copies[j].wait_recv()
        grad_own = grad_own + grad_recv[j].astype(f32)
    grad_ref[...] = grad_own
    for c in copies:
        c.wait_send()


def body(
    grid_x, mesh_h, w_in, w_q, w_kv, w_o, w_pqkv, w_po, edge_src, edge_dst, edge_count, win_idx, cot
):
    n_grid = lax.axis_size("grid")
    n_head = lax.axis_size("head")
    n_group = lax.axis_size("groups")
    cols = w_q.shape[1]
    nodes, width = mesh_h.shape
    cap = edge_src.shape[2]
    channels = grid_x.shape[1]
    own = nodes // n_head
    chunk = width // n_grid
    slots = n_grid * cap
    padded = channels + (-channels % 16)
    vmem = pl.BlockSpec(memory_space=pltpu.VMEM)
    hm, grad = pl.pallas_call(
        functools.partial(kernel, n_grid, n_head, n_group),
        out_shape=(
            jax.ShapeDtypeStruct((nodes, cols), f32),
            jax.ShapeDtypeStruct((chunk, 2 * cols), f32),
        ),
        in_specs=[vmem] * 13,
        out_specs=(vmem, vmem),
        scratch_shapes=[
            pltpu.VMEM((2 * n_grid - 1, padded, cap), bf16),
            pltpu.VMEM((width, slots + nodes), bf16),
            pltpu.VMEM((n_grid, cap, nodes), bf16),
            pltpu.VMEM((n_grid, nodes, cap), bf16),
            pltpu.VMEM((n_grid, cap, 2 * cols), bf16),
            pltpu.VMEM((n_grid, cap, cols), f32),
            pltpu.VMEM((n_grid, cap, cols), f32),
            pltpu.VMEM((slots + nodes, 2 * cols), bf16),
            pltpu.VMEM((nodes, cols), bf16),
            pltpu.VMEM((nodes, 2 * cols), bf16),
            pltpu.VMEM((nodes, nodes), f32),
            pltpu.VMEM((width, 2 * cols), bf16),
            pltpu.VMEM((padded, width), bf16),
            pltpu.VMEM((n_grid, cap), jnp.int32),
            pltpu.VMEM((n_head * cols, width), bf16),
            pltpu.VMEM((n_head, nodes, cols), bf16),
            pltpu.VMEM((nodes, width), f32),
            pltpu.VMEM((n_head, nodes, cols), bf16),
            pltpu.VMEM((n_head - 1, nodes, cols), bf16),
            pltpu.VMEM((nodes, width), bf16),
            pltpu.VMEM((n_head - 1, own, width), bf16),
            pltpu.VMEM((n_head, own, cols), bf16),
            pltpu.VMEM((nodes, cols), bf16),
            pltpu.VMEM((n_grid // 2, chunk, 2 * cols), bf16),
            pltpu.VMEM((n_grid // 2, chunk, 2 * cols), bf16),
            pltpu.VMEM((n_grid // 2 - 1, chunk, 2 * cols), bf16),
            pltpu.VMEM((n_grid // 2 - 1, chunk, 2 * cols), bf16),
            pltpu.SemaphoreType.DMA((4, n_head - 1)),
            pltpu.SemaphoreType.DMA((4, n_head - 1)),
            pltpu.SemaphoreType.DMA((2, n_grid - 1)),
            pltpu.SemaphoreType.DMA((2, n_grid - 1)),
            pltpu.SemaphoreType.DMA((n_head - 1,)),
            pltpu.SemaphoreType.DMA((n_head - 1,)),
            pltpu.SemaphoreType.DMA((n_group - 1, n_head - 1)),
            pltpu.SemaphoreType.DMA((n_group - 1, n_head - 1)),
            pltpu.SemaphoreType.DMA((n_group, n_head - 1)),
            pltpu.SemaphoreType.DMA((n_group, n_head - 1)),
            pltpu.SemaphoreType.DMA((n_grid // 2,)),
            pltpu.SemaphoreType.DMA((n_grid // 2,)),
        ],
        compiler_params=pltpu.CompilerParams(
            collective_id=0, has_side_effects=True, vmem_limit_bytes=56 * 1024 * 1024
        ),
    )(
        grid_x.T,
        mesh_h,
        w_in,
        w_q,
        w_kv,
        w_o,
        w_pqkv.transpose(1, 0, 2),
        w_po,
        edge_src,
        edge_dst,
        edge_count,
        win_idx.T,
        cot,
    )
    return hm.astype(bf16), grad.reshape(chunk, 2, cols)


def solution(mesh):
    placed = (
        P(("groups", "grid"), None),
        P(("groups", "grid"), None),
        P(),
        P(None, "head"),
        P(None, None, "head"),
        P("head", None),
        P(None, None, "head"),
        P("head", None),
        P("grid", None, None),
        P("grid", None, None),
        P("grid", None),
        P("grid", None),
        P(("groups", "grid"), None),
    )
    return jax.shard_map(
        body,
        mesh=mesh,
        in_specs=placed,
        out_specs=(P(("groups", "grid"), "head"), P(("groups", "grid"), None, "head")),
        check_vma=False,
    )
```
